512 devices in a mesh: row: 16 (over y, x), col: 32 (over z, core).
Axes of the slice: x: 4, y: 4, z: 16, core: 2. Of those that a mesh axis runs over, the one named last changes fastest.
Arguments:
- points: float32 [8, 65536], P(None, ('row', 'col')), may hold values from -6 to 6
- lengthscale: float32 [8], replicated, may hold values from 1.5 to 4
- signal_var: float32 [1], replicated, may hold values from 0.002 to 0.01
- noise_var: float32 [1], replicated, may hold values from 0.3 to 1.5
- solution: float32 [4, 65536], P(None, ('row', 'col')), may hold values from -6 to 6
- residual: float32 [4, 65536], P(None, ('row', 'col')), may hold values from -30 to 30, as said below
- direction: float32 [4, 65536], P(None, ('row', 'col')), may hold values from -6 to 6
Outputs:
- new_solution: float32 [4, 65536], P(None, ('row', 'col'))
- new_residual: float32 [4, 65536], P(None, ('row', 'col'))
- new_direction: float32 [4, 65536], P(None, ('row', 'col'))
The draws below stay inside these ranges and needn't reach their ends.
Inputs may be any that keep to these rules, and one draw needn't show every extreme that they name: residual values, real-valued.
All inputs are finite; a program needn't handle non-finite values.
Results may differ from the reference program's by a relative error of at most 0.00017.
Values sent between devices are 32-bit elements; how exact they have to be, the bound alone decides.
No kernel may reach another device: no remote copies, remote signals or barrier semaphores. Data moves between devices by JAX's collectives and lax.ppermute only.
A program may use at most 128 MiB of HBM per device.

```python
import math
import jax
import jax.numpy as jnp
from jax import lax

DIM = 8
RHS = 4
NPTS = 65536


def draw_residual(key, part):
    key = jax.random.fold_in(key, 5)
    first, second = jax.random.split(key)
    spread = jnp.exp(jax.random.uniform(second, (RHS, NPTS), jnp.float32) * jnp.log(10.0))
    ramp = 1.0 + 2.0 * jnp.arange(NPTS, dtype=jnp.float32) / NPTS
    base = jnp.clip(jax.random.normal(first, (RHS, NPTS), jnp.float32), -4.0, 4.0)
    return base * spread * ramp[None, :] * 0.25


def level_of(own_key, shape, shards, smallest, largest):
    def one(position, shards_of):
        steps = jax.random.uniform(jax.random.fold_in(jax.random.fold_in(own_key, 6), position), (shards_of,), jnp.float32, smallest / len(shards), largest / len(shards))
        return jnp.repeat(jnp.exp(steps), shape[position] // shards_of).reshape((-1,) + (1,) * (len(shape) - position - 1))

    gain = one(*shards[0])
    for cut in shards[1:]:
        gain = gain * one(*cut)
    return gain


def bell_draw(own_key, extent, scale, reach, cuts=(), held_as=jnp.bfloat16):
    array = jax.random.normal(own_key, extent, jnp.float32) * scale
    if len(cuts) > 0:
        array = level_of(own_key, extent, cuts, -0.22, 0.18) * array
    return jnp.clip(array, min=-reach, max=reach).astype(held_as)


def setup_inputs(seed: int = 0) -> dict:
    streams_of = jax.random.split(jax.random.key(seed), 8)
    return {
        "points": bell_draw(streams_of[0], (DIM, NPTS), 1.0, 6.0, ((1, 512),), jnp.float32),
        "lengthscale": jnp.clip(jnp.exp(jax.random.uniform(streams_of[1], (DIM,), jnp.float32, math.log(1.5), math.log(4.0))), 1.5, 4.0),
        "signal_var": jnp.clip(jnp.exp(jax.random.uniform(streams_of[2], (1,), jnp.float32, math.log(0.002), math.log(0.01))), 0.002, 0.01),
        "noise_var": jnp.clip(jax.random.uniform(streams_of[3], (1,), jnp.float32, 0.3, 1.5), 0.3, 1.5),
        "solution": bell_draw(streams_of[4], (RHS, NPTS), 1.0, 6.0, ((1, 512),), jnp.float32),
        "residual": draw_residual(jax.random.fold_in(streams_of[7], 71), 0),
        "direction": bell_draw(streams_of[6], (RHS, NPTS), 1.0, 6.0, ((1, 512),), jnp.float32),
    }


def kernel_apply(row_pts, col_pts, col_dir, scale):
    rows = row_pts.shape[1]
    block = min(256, rows)
    blocks = row_pts.reshape(row_pts.shape[0], rows // block, block).transpose(1, 0, 2)

    def one_block(left):
        dist_sq = jnp.zeros((left.shape[1], col_pts.shape[1]), jnp.float32)
        for dim_idx in range(left.shape[0]):
            delta = left[dim_idx][:, None] - col_pts[dim_idx][None, :]
            dist_sq = dist_sq + delta * delta
        radius = jnp.sqrt(dist_sq)
        root_five = jnp.sqrt(jnp.float32(5.0))
        values = scale * (1.0 + root_five * radius + 5.0 / 3.0 * dist_sq) * jnp.exp(-root_five * radius)
        return jnp.einsum('rc,kc->kr', values, col_dir, precision=lax.Precision.HIGHEST)
    result = lax.map(one_block, blocks)
    return result.transpose(1, 0, 2).reshape(col_dir.shape[0], rows)

def reference(points, lengthscale, signal_var, noise_var, solution, residual, direction):
    scaled = points / lengthscale[:, None]
    image = kernel_apply(scaled, scaled, direction, signal_var[0]) + noise_var[0] * direction
    old_rr = lax.optimization_barrier(jnp.sum(residual * residual, axis=1))
    curv = lax.optimization_barrier(jnp.sum(direction * image, axis=1))
    alpha = old_rr / curv
    new_solution = solution + alpha[:, None] * direction
    new_residual = residual - alpha[:, None] * image
    new_rr = lax.optimization_barrier(jnp.sum(new_residual * new_residual, axis=1))
    new_direction = new_residual + (new_rr / old_rr)[:, None] * direction
    return (new_solution, new_residual, new_direction)
```

```python
import functools
import math

import jax
import jax.numpy as jnp
from jax import lax
from jax.experimental import pallas as pl
from jax.experimental.pallas import tpu as pltpu
from jax.sharding import Mesh, PartitionSpec as P

BLK = 128
LN2 = math.log(2.0)
UNIT = math.sqrt(5.0) / LN2
HALF = 1.5 / LN2
REST = 3.0 / LN2**2 - HALF**2
FRONT = LN2**2 / 3.0
TINY = 1e-12
FEAT = 64


def round16(x):
    return x.astype(jnp.bfloat16).astype(jnp.float32)


def split3(x):
    first = round16(x)
    rest = x - first
    second = round16(rest)
    return first, second, round16(rest - second)


def norm_rows(pts, flip):
    parts = split3(jnp.sum(pts * pts, axis=0, keepdims=True))
    row = lax.broadcasted_iota(jnp.int32, pts.shape, 0)
    at = 3 if flip else 0
    out = jnp.where((row >= 3 - at) & (row < 6 - at), 1.0, 0.0)
    for k in range(3):
        out = jnp.where(row == at + k, parts[k], out)
    return out


def out_features(pts):
    a, b, c = split3(pts)
    return jnp.concatenate([a, b, c, a, b, a, norm_rows(pts, False), jnp.zeros_like(pts)], 0)


def in_features(pts):
    a, b, c = split3(-2.0 * pts)
    return jnp.concatenate([a, a, a, b, b, c, norm_rows(pts, True), jnp.zeros_like(pts)], 0)


def product_kernel(tb, sb, s_ref, t_ref, out_ref, g_ref, f_ref, d_ref, acc_ref):
    n_s, n_t = s_ref.shape[0], t_ref.shape[0]
    for k in range(n_s):
        g_ref[:, k * BLK : (k + 1) * BLK] = out_features(s_ref[k, :8, :]).astype(jnp.bfloat16)
    for k in range(n_t):
        at = slice(k * BLK, (k + 1) * BLK)
        rows = in_features(t_ref[k, :8, :])
        f_ref[at, :] = jnp.transpose(rows).astype(jnp.bfloat16)
        a, b, c = split3(t_ref[k, 8:12, :])
        d_ref[:, at] = jnp.concatenate([a, b, c, jnp.zeros_like(a)], 0).astype(jnp.bfloat16)
    acc_ref[...] = jnp.zeros_like(acc_ref)

    def step(i, carry):
        t_at = pl.ds(pl.multiple_of(i * tb, tb), tb)
        left = f_ref[t_at, :]
        weights = d_ref[:, t_at]
        for j in range(n_s * BLK // sb):
            s_at = slice(j * sb, (j + 1) * sb)
            d2 = jnp.dot(left, g_ref[:, s_at], preferred_element_type=jnp.float32)
            d2 = jnp.maximum(d2, TINY)
            neg = -(d2 * lax.rsqrt(d2))
            shifted = neg - HALF
            value = (shifted * shifted + REST) * jnp.exp2(neg)
            high = value.astype(jnp.bfloat16)
            low = (value - high.astype(jnp.float32)).astype(jnp.bfloat16)
            acc_ref[:, s_at] += jnp.dot(
                weights, high, preferred_element_type=jnp.float32
            ) + jnp.dot(weights, low, preferred_element_type=jnp.float32)
        return carry

    lax.fori_loop(0, n_t * BLK // tb, step, 0)
    total = acc_ref[0:4, :] + acc_ref[4:8, :] + acc_ref[8:12, :]
    for k in range(n_s):
        out_ref[k, :, :] = total[:, k * BLK : (k + 1) * BLK]


def kernel_product(s_blocks, t_blocks, tb=256, sb=512):
    n_s, n_t = s_blocks.shape[0], t_blocks.shape[0]
    return pl.pallas_call(
        functools.partial(product_kernel, tb, sb),
        out_shape=jax.ShapeDtypeStruct((n_s, 4, BLK), jnp.float32),
        in_specs=[pl.BlockSpec(memory_space=pltpu.VMEM)] * 2,
        out_specs=pl.BlockSpec(memory_space=pltpu.VMEM),
        scratch_shapes=[
            pltpu.VMEM((FEAT, n_s * BLK), jnp.bfloat16),
            pltpu.VMEM((n_t * BLK, FEAT), jnp.bfloat16),
            pltpu.VMEM((16, n_t * BLK), jnp.bfloat16),
            pltpu.VMEM((16, n_s * BLK), jnp.float32),
        ],
        compiler_params=pltpu.CompilerParams(vmem_limit_bytes=32 * 1024 * 1024),
    )(s_blocks, t_blocks)


def tiled(x, n):
    return jnp.broadcast_to(x[None], (n,) + x.shape)


def on_device(points, lengthscale, signal_var, noise_var, solution, residual, direction):
    scaled = points / lengthscale[:, None] * UNIT
    mine = jnp.concatenate([scaled, direction, residual], 0)
    with jax.named_scope("gather_out_points"):
        s_blocks = lax.all_to_all(tiled(mine, 16), "row", 0, 0)
    with jax.named_scope("gather_in_points"):
        t_half = lax.all_to_all(tiled(mine[:12], 16), "z", 0, 0)
        t_other = lax.ppermute(t_half, "core", [(0, 1), (1, 0)])
    part = kernel_product(s_blocks, jnp.concatenate([t_half, t_other], 0))
    with jax.named_scope("sum_partial_images"):
        applied = jnp.sum(lax.all_to_all(tiled(part, 16), "row", 0, 0), 0)
    s_dir, s_res = s_blocks[:, 8:12], s_blocks[:, 12:16]
    image = (signal_var[0] * FRONT) * applied + noise_var[0] * s_dir
    sums = jnp.concatenate(
        [
            jnp.sum(u * v, (0, 2))
            for u, v in ((s_res, s_res), (s_dir, image), (s_res, image), (image, image))
        ]
    )
    with jax.named_scope("sum_scalars"):
        sums = lax.all_to_all(tiled(jnp.pad(sums, (0, 112))[None], 32), ("z", "core"), 0, 0)
    sums = jnp.sum(sums, (0, 1))
    old_rr, curv, res_image, image_sq = (sums[4 * k : 4 * k + 4, None] for k in range(4))
    own = lax.dynamic_index_in_dim(image, lax.axis_index("row"), 0, False)
    alpha = old_rr / curv
    new_rr = old_rr - 2.0 * alpha * res_image + alpha * alpha * image_sq
    new_solution = solution + alpha * direction
    new_residual = residual - alpha * own
    new_direction = new_residual + (new_rr / old_rr) * direction
    return new_solution, new_residual, new_direction


def solution(mesh):
    fine = Mesh(mesh.devices.reshape(16, 16, 2), ("row", "z", "core"))
    cut = P(None, ("row", "z", "core"))
    return jax.shard_map(
        on_device,
        mesh=fine,
        in_specs=(cut, P(), P(), P(), cut, cut, cut),
        out_specs=(cut, cut, cut),
        check_vma=False,
    )
```

```python
import functools
import math

import jax
import jax.numpy as jnp
from jax import lax
from jax.experimental import pallas as pl
from jax.experimental.pallas import tpu as pltpu
from jax.sharding import Mesh, PartitionSpec as P

BLK = 128
LN2 = math.log(2.0)
UNIT = math.sqrt(5.0) / LN2
HALF = 1.5 / LN2
REST = 3.0 / LN2**2 - HALF**2
FRONT = LN2**2 / 3.0
TINY = 1e-12
FEAT = 64
QUARTER = 16
S_TILE = 256


def round16(x):
    return x.astype(jnp.bfloat16).astype(jnp.float32)


def split3(x):
    first = round16(x)
    rest = x - first
    second = round16(rest)
    return first, second, round16(rest - second)


def norm_rows(pts, flip):
    parts = split3(jnp.sum(pts * pts, axis=0, keepdims=True))
    row = lax.broadcasted_iota(jnp.int32, pts.shape, 0)
    at = 3 if flip else 0
    out = jnp.where((row >= 3 - at) & (row < 6 - at), 1.0, 0.0)
    for k in range(3):
        out = jnp.where(row == at + k, parts[k], out)
    return out


def out_features(pts):
    a, b, c = split3(pts)
    return jnp.concatenate([a, b, c, a, b, a, norm_rows(pts, False), jnp.zeros_like(pts)], 0)


def in_features(pts):
    a, b, c = split3(-2.0 * pts)
    return jnp.concatenate([a, a, a, b, b, c, norm_rows(pts, True), jnp.zeros_like(pts)], 0)


def product_kernel(first, last, y_ref, s_ref, t_ref, prior_ref, out_ref, g_ref, f_ref, d_ref, acc_ref):
    n_s = s_ref.shape[0]
    for k in range(n_s):
        g_ref[:, k * BLK : (k + 1) * BLK] = out_features(s_ref[k, :8, :]).astype(jnp.bfloat16)
    acc_ref[...] = jnp.zeros_like(acc_ref)
    me = y_ref[0]

    def step(i, carry):
        quarter = lax.rem(me + i, t_ref.shape[0])
        for k in range(QUARTER):
            at = slice(k * BLK, (k + 1) * BLK)
            rows = in_features(t_ref[quarter, k, :8, :])
            f_ref[at, :] = jnp.transpose(rows).astype(jnp.bfloat16)
            a, b, c = split3(t_ref[quarter, k, 8:12, :])
            d_ref[:, at] = jnp.concatenate([a, b, c, jnp.zeros_like(a)], 0).astype(jnp.bfloat16)
        left = f_ref[...]
        weights = d_ref[...]
        for j in range(n_s * BLK // S_TILE):
            at = slice(j * S_TILE, (j + 1) * S_TILE)
            d2 = jnp.dot(left, g_ref[:, at], preferred_element_type=jnp.float32)
            d2 = jnp.maximum(d2, TINY)
            neg = -(d2 * lax.rsqrt(d2))
            shifted = neg - HALF
            value = (shifted * shifted + REST) * jnp.exp2(neg)
            high = value.astype(jnp.bfloat16)
            low = (value - high.astype(jnp.float32)).astype(jnp.bfloat16)
            acc_ref[:, at] += jnp.dot(
                weights, high, preferred_element_type=jnp.float32
            ) + jnp.dot(weights, low, preferred_element_type=jnp.float32)
        return carry

    lax.fori_loop(first, last, step, 0)
    total = acc_ref[0:4, :] + acc_ref[4:8, :] + acc_ref[8:12, :]
    for k in range(n_s):
        out_ref[k, :, :] = prior_ref[k, :, :] + total[:, k * BLK : (k + 1) * BLK]


def kernel_product(me, s_blocks, t_blocks, prior, first, last):
    n_s = s_blocks.shape[0]
    entries = (last - first) * QUARTER * BLK * n_s * BLK
    return pl.pallas_call(
        functools.partial(product_kernel, first, last),
        out_shape=jax.ShapeDtypeStruct((n_s, 4, BLK), jnp.float32),
        in_specs=[pl.BlockSpec(memory_space=pltpu.SMEM)]
        + [pl.BlockSpec(memory_space=pltpu.VMEM)] * 3,
        out_specs=pl.BlockSpec(memory_space=pltpu.VMEM),
        scratch_shapes=[
            pltpu.VMEM((FEAT, n_s * BLK), jnp.bfloat16),
            pltpu.VMEM((QUARTER * BLK, FEAT), jnp.bfloat16),
            pltpu.VMEM((16, QUARTER * BLK), jnp.bfloat16),
            pltpu.VMEM((16, n_s * BLK), jnp.float32),
        ],
        compiler_params=pltpu.CompilerParams(vmem_limit_bytes=40 * 1024 * 1024),
        cost_estimate=pl.CostEstimate(
            flops=entries * 192, bytes_accessed=0, transcendentals=entries * 2
        ),
    )(me, s_blocks, t_blocks, prior)


def tiled(x, n):
    return jnp.broadcast_to(x[None], (n,) + x.shape)


AXIS = "d"
YS, XS, ZS, CS = (2, 3, 0, 1), (2, 3, 0, 1), tuple((8 + k) % 16 for k in range(16)), (0, 1)


def flat(y, x, z, c):
    return ((y * 4 + x) * 16 + z) * 2 + c


ALONG_Z = [[flat(y, x, z, c) for z in ZS] for y in YS for x in XS for c in CS]
ALONG_Y = [[flat(y, x, z, c) for y in YS] for x in XS for z in ZS for c in CS]
ALONG_XC = [[flat(y, x, z, c) for x in XS for c in CS] for y in YS for z in ZS]
ALONG_YZ = [[flat(y, x, z, c) for y in YS for z in ZS] for x in XS for c in CS]
EVERY = [(y, x, z, c) for y in range(4) for x in range(4) for z in range(16) for c in range(2)]


def share(x, groups):
    return lax.all_to_all(x, AXIS, 0, 0, axis_index_groups=groups)


def shift_x(v, by):
    return lax.ppermute(
        v, AXIS, [(flat(y, x, z, c), flat(y, (x - by) % 4, z, c)) for y, x, z, c in EVERY]
    )


def swap_core(v):
    return lax.ppermute(v, AXIS, [(i, i ^ 1) for i in range(512)])


def on_device(points, lengthscale, signal_var, noise_var, solution, residual, direction):
    here = lax.axis_index(AXIS)
    at_y, at_x, core = here // 128, here // 32 % 4, here % 2
    scaled = points / lengthscale[:, None] * UNIT
    mine = jnp.concatenate([scaled, direction, residual], 0)
    with jax.named_scope("gather_in_points_z"):
        t_quarter = share(tiled(mine[:12], 16), ALONG_Z)
    with jax.named_scope("gather_out_points"):
        row = jnp.stack([mine] + [shift_x(mine, k) for k in (1, 2, 3)])
        row = jnp.roll(row, at_x, 0)
        swapped = swap_core(row)
        s_blocks = jnp.concatenate(
            [jnp.where(core == 0, row, swapped), jnp.where(core == 0, swapped, row)], 0
        )
    with jax.named_scope("gather_in_points_y"):
        t_all = share(tiled(t_quarter, 4), ALONG_Y)
    me = (at_y + 2)[None] % 4
    part = kernel_product(
        jnp.zeros_like(me), s_blocks, t_quarter[None], jnp.zeros((8, 4, BLK), jnp.float32), 0, 1
    )
    part = kernel_product(me, s_blocks, t_all, part, 1, 4)
    with jax.named_scope("sum_partial_images"):
        applied = jnp.sum(share(tiled(part, 8), ALONG_XC), 0)
    s_dir, s_res = s_blocks[:, 8:12], s_blocks[:, 12:16]
    image = (signal_var[0] * FRONT) * applied + noise_var[0] * s_dir
    sums = jnp.concatenate(
        [
            jnp.sum(u * v, (0, 2))
            for u, v in ((s_res, s_res), (s_dir, image), (s_res, image), (image, image))
        ]
    )
    with jax.named_scope("sum_scalars"):
        sums = share(tiled(jnp.pad(sums, (0, 112))[None], 64), ALONG_YZ)
    sums = jnp.sum(sums, (0, 1))
    old_rr, curv, res_image, image_sq = (sums[4 * k : 4 * k + 4, None] for k in range(4))
    own = lax.dynamic_index_in_dim(image, core * 4 + at_x, 0, False)
    alpha = old_rr / curv
    new_rr = old_rr - 2.0 * alpha * res_image + alpha * alpha * image_sq
    new_solution = solution + alpha * direction
    new_residual = residual - alpha * own
    new_direction = new_residual + (new_rr / old_rr) * direction
    return new_solution, new_residual, new_direction


def solution(mesh):
    line = Mesh(mesh.devices.reshape(-1), (AXIS,))
    cut = P(None, AXIS)
    return jax.shard_map(
        on_device,
        mesh=line,
        in_specs=(cut, P(), P(), P(), cut, cut, cut),
        out_specs=(cut, cut, cut),
        check_vma=False,
    )
```

```python
import functools
import math

import jax
import jax.numpy as jnp
from jax import lax
from jax.experimental import pallas as pl
from jax.experimental.pallas import tpu as pltpu
from jax.sharding import Mesh, PartitionSpec as P

BLK = 128
LN2 = math.log(2.0)
UNIT = math.sqrt(5.0) / LN2
HALF = 1.5 / LN2
REST = 3.0 / LN2**2 - HALF**2
FRONT = LN2**2 / 3.0 * 2.0**HALF
TINY = 1e-12
FEAT = 64
S_TILE = 256
T_STEP = 4096
T_TILE = 256


def round16(x):
    return x.astype(jnp.bfloat16).astype(jnp.float32)


def split3(x):
    first = round16(x)
    rest = x - first
    second = round16(rest)
    return first, second, round16(rest - second)


def norm_rows(pts, flip):
    parts = split3(jnp.sum(pts * pts, axis=0, keepdims=True))
    row = lax.broadcasted_iota(jnp.int32, pts.shape, 0)
    at = 3 if flip else 0
    out = jnp.where((row >= 3 - at) & (row < 6 - at), 1.0, 0.0)
    for k in range(3):
        out = jnp.where(row == at + k, parts[k], out)
    return out


def out_features(pts):
    a, b, c = split3(pts)
    return jnp.concatenate([a, b, c, a, b, a, norm_rows(pts, False), jnp.zeros_like(pts)], 0)


def in_features(pts):
    a, b, c = split3(-2.0 * pts)
    return jnp.concatenate([a, a, a, b, b, c, norm_rows(pts, True), jnp.zeros_like(pts)], 0)


def prepare_kernel(own_ref, other_ref, f_ref, d_ref):
    for half, ref in enumerate((own_ref, other_ref)):
        for k in range(16):
            at = slice((half * 16 + k) * BLK, (half * 16 + k + 1) * BLK)
            rows = in_features(jnp.concatenate([ref[k, 0], ref[k, 1]], 0))
            f_ref[at, :] = jnp.transpose(rows).astype(jnp.bfloat16)
            a, b, c = split3(ref[k, 2])
            d_ref[:, at] = jnp.concatenate([a, b, c, jnp.zeros_like(a)], 0).astype(jnp.bfloat16)


def product_kernel(f_ref, d_ref, s_ref, out_ref, g_ref, acc_ref):
    n_s = s_ref.shape[0]
    for k in range(n_s):
        g_ref[:, k * BLK : (k + 1) * BLK] = out_features(s_ref[k, :8, :]).astype(jnp.bfloat16)
    acc_ref[...] = jnp.zeros_like(acc_ref)

    def step(i, carry):
        rows = pl.ds(pl.multiple_of(i * T_STEP, T_STEP), T_STEP)
        for j in range(n_s * BLK // S_TILE):
            at = slice(j * S_TILE, (j + 1) * S_TILE)
            total = acc_ref[:, at]
            for t in range(T_STEP // T_TILE):
                here = pl.ds(pl.multiple_of(i * T_STEP + t * T_TILE, T_TILE), T_TILE)
                d2 = jnp.dot(f_ref[here, :], g_ref[:, at], preferred_element_type=jnp.float32)
                d2 = jnp.maximum(d2, TINY)
                neg = -HALF - d2 * lax.rsqrt(d2)
                value = (neg * neg + REST) * jnp.exp2(neg)
                high = value.astype(jnp.bfloat16)
                low = (value - high.astype(jnp.float32)).astype(jnp.bfloat16)
                weights = d_ref[:, here]
                total = total + (
                    jnp.dot(weights, high, preferred_element_type=jnp.float32)
                    + jnp.dot(weights, low, preferred_element_type=jnp.float32)
                )
            acc_ref[:, at] = total
        return carry

    lax.fori_loop(0, f_ref.shape[0] // T_STEP, step, 0)
    total = acc_ref[0:4, :] + acc_ref[4:8, :] + acc_ref[8:12, :]
    for k in range(n_s):
        for to in range(n_s):
            out_ref[to, k, :, :] = total[:, k * BLK : (k + 1) * BLK]


def to_lanes(column):
    row = lax.broadcasted_iota(jnp.int32, (16, BLK), 0)
    lane = lax.broadcasted_iota(jnp.int32, (16, BLK), 1)
    return jnp.sum(jnp.where(row == lane, column, 0.0), axis=0, keepdims=True)


def to_column(lanes):
    row = lax.broadcasted_iota(jnp.int32, (16, BLK), 0)
    lane = lax.broadcasted_iota(jnp.int32, (16, BLK), 1)
    return jnp.sum(jnp.where(row == lane, lanes, 0.0), axis=1, keepdims=True)


def start_kernel(ls_ref, pts_ref, res_ref, dir_ref, to_yx_ref, to_z_ref, ls, pts, res, direct, sems):
    copies = [
        pltpu.make_async_copy(source, target, sems.at[k])
        for k, (source, target) in enumerate(
            ((ls_ref, ls), (pts_ref, pts), (dir_ref, direct), (res_ref, res))
        )
    ]
    for copy in copies:
        copy.start()
    for copy in copies:
        copy.wait()
    row = lax.broadcasted_iota(jnp.int32, (8, 8), 0)
    lane = lax.broadcasted_iota(jnp.int32, (8, 8), 1)
    scale = jnp.sum(jnp.where(row == lane, ls[...], 0.0), axis=1, keepdims=True)
    scaled = pts[...] / scale * UNIT
    direction, residual = direct[...], res[...]
    for k in range(16):
        to_yx_ref[k, 0:8, :] = scaled
        to_yx_ref[k, 8:12, :] = direction
        to_yx_ref[k, 12:16, :] = residual
        to_z_ref[k, 0] = scaled[0:4]
        to_z_ref[k, 1] = scaled[4:8]
        to_z_ref[k, 2] = direction


def sums_kernel(at_ref, sv_ref, nv_ref, parts_ref, s_ref, own_ref, out_ref, image_ref):
    front, noise = sv_ref[0] * FRONT, nv_ref[0]
    rr, curv, cross, square = (jnp.zeros((4, BLK), jnp.float32) for _ in range(4))
    for k in range(16):
        applied = parts_ref[0, k]
        for source in range(1, 16):
            applied = applied + parts_ref[source, k]
        s_dir, s_res = s_ref[k, 8:12, :], s_ref[k, 12:16, :]
        image = front * applied + noise * s_dir
        image_ref[k] = image
        rr, curv = rr + s_res * s_res, curv + s_dir * image
        cross, square = cross + s_res * image, square + image * image
    own_ref[...] = image_ref[at_ref[0]]
    column = jnp.sum(jnp.concatenate([rr, curv, cross, square], 0), axis=1, keepdims=True)
    lanes = to_lanes(column)
    for to in range(32):
        out_ref[to] = lanes


def end_kernel(sums_ref, own_ref, sol_ref, res_ref, dir_ref, new_sol_ref, new_res_ref, new_dir_ref):
    total = sums_ref[0]
    for k in range(1, 32):
        total = total + sums_ref[k]
    column = to_column(total)
    old_rr, curv, cross, square = (column[4 * k : 4 * k + 4] for k in range(4))
    alpha = old_rr / curv
    new_rr = old_rr - 2.0 * alpha * cross + alpha * alpha * square
    direction = dir_ref[...]
    new_residual = res_ref[...] - alpha * own_ref[...]
    new_sol_ref[...] = sol_ref[...] + alpha * direction
    new_res_ref[...] = new_residual
    new_dir_ref[...] = new_residual + (new_rr / old_rr) * direction


def call(body, shapes, where, scratch=(), entries=0, limit=40):
    spec = {
        "s": pl.BlockSpec(memory_space=pltpu.SMEM),
        "v": pl.BlockSpec(memory_space=pltpu.VMEM),
        "a": pl.BlockSpec(memory_space=pl.ANY),
    }
    return pl.pallas_call(
        body,
        out_shape=[jax.ShapeDtypeStruct(s, t) for s, t in shapes],
        in_specs=[spec[w] for w in where],
        out_specs=[pl.BlockSpec(memory_space=pltpu.VMEM) for _ in shapes],
        scratch_shapes=[x if hasattr(x, "dtype") else pltpu.VMEM(*x) for x in scratch],
        compiler_params=pltpu.CompilerParams(vmem_limit_bytes=limit * 1024 * 1024),
        cost_estimate=pl.CostEstimate(
            flops=entries * 192, bytes_accessed=0, transcendentals=entries * 2
        ),
    )


AXIS = "d"
YS, XS, ZS, CS = (2, 3, 0, 1), (2, 3, 0, 1), tuple((8 + k) % 16 for k in range(16)), (0, 1)


def flat(y, x, z, c):
    return ((y * 4 + x) * 16 + z) * 2 + c


ALONG_Z = [[flat(y, x, z, c) for z in ZS] for y in YS for x in XS for c in CS]
ALONG_YX = [[flat(y, x, z, c) for y in YS for x in XS] for z in ZS for c in CS]
ALONG_ZC = [[flat(y, x, z, c) for z in ZS for c in CS] for y in YS for x in XS]


def share(x, groups):
    return lax.all_to_all(x, AXIS, 0, 0, axis_index_groups=groups)


def on_device(points, lengthscale, signal_var, noise_var, solution, residual, direction):
    f32, bf16 = jnp.float32, jnp.bfloat16
    here = lax.axis_index(AXIS)
    place = ((here // 128 + 2) % 4 * 4 + (here // 32 + 2) % 4)[None]
    to_yx, to_z = call(
        start_kernel,
        [((16, 16, BLK), f32), ((16, 3, 4, BLK), f32)],
        "aaaa",
        [((1, 8), f32), ((8, BLK), f32), ((4, BLK), f32), ((4, BLK), f32), pltpu.SemaphoreType.DMA((4,))],
        limit=60,
    )(lengthscale[None], points, residual, direction)
    with jax.named_scope("gather_in_points"):
        t_own = share(to_z, ALONG_Z)
        t_other = lax.ppermute(t_own, AXIS, [(i, i ^ 1) for i in range(512)])
    with jax.named_scope("gather_out_points"):
        s_blocks = share(to_yx, ALONG_YX)
    n_t, n_s = 32 * BLK, 16 * BLK
    rows, weights = call(
        prepare_kernel, [((n_t, FEAT), bf16), ((16, n_t), bf16)], "vv", entries=n_t * 256
    )(t_own, t_other)
    (parts,) = call(
        product_kernel,
        [((16, 16, 4, BLK), f32)],
        "vvv",
        [((FEAT, n_s), bf16), ((16, n_s), f32)],
        n_t * n_s,
    )(rows, weights, s_blocks)
    with jax.named_scope("sum_partial_images"):
        parts = share(parts, ALONG_YX)
    own, to_zc = call(
        sums_kernel, [((4, BLK), f32), ((32, 1, BLK), f32)], "sssvv", [((16, 4, BLK), f32)]
    )(place, signal_var, noise_var, parts, s_blocks)
    with jax.named_scope("sum_scalars"):
        sums = share(to_zc, ALONG_ZC)
    return tuple(
        call(end_kernel, [((4, BLK), f32)] * 3, "vvvvv")(sums, own, solution, residual, direction)
    )


def solution(mesh):
    line = Mesh(mesh.devices.reshape(-1), (AXIS,))
    cut = P(None, AXIS)
    return jax.shard_map(
        on_device,
        mesh=line,
        in_specs=(cut, P(), P(), P(), cut, cut, cut),
        out_specs=(cut, cut, cut),
        check_vma=False,
    )
```

```python
import functools
import math

import jax
import jax.numpy as jnp
from jax import lax
from jax.experimental import pallas as pl
from jax.experimental.pallas import tpu as pltpu
from jax.sharding import Mesh, PartitionSpec as P

BLK = 128
LN2 = math.log(2.0)
UNIT = math.sqrt(5.0) / LN2
HALF = 1.5 / LN2
REST = 3.0 / LN2**2 - HALF**2
FRONT = LN2**2 / 3.0 * 2.0**HALF
FEAT = 64
S_TILE = 256
T_STEP = 4096
T_TILE = 256


def round16(x):
    return x.astype(jnp.bfloat16).astype(jnp.float32)


def split3(x):
    first = round16(x)
    rest = x - first
    second = round16(rest)
    return first, second, round16(rest - second)


def norm_rows(pts, flip):
    parts = split3(jnp.sum(pts * pts, axis=0, keepdims=True))
    row = lax.broadcasted_iota(jnp.int32, pts.shape, 0)
    at = 3 if flip else 0
    out = jnp.where((row >= 3 - at) & (row < 6 - at), 1.0, 0.0)
    for k in range(3):
        out = jnp.where(row == at + k, parts[k], out)
    return out


def out_features(pts):
    a, b, c = split3(pts)
    return jnp.concatenate([a, b, c, a, b, a, norm_rows(pts, False), jnp.zeros_like(pts)], 0)


def in_features(pts):
    a, b, c = split3(-2.0 * pts)
    return jnp.concatenate([a, a, a, b, b, c, norm_rows(pts, True), jnp.zeros_like(pts)], 0)


def prepare_kernel(own_ref, other_ref, f_ref, d_ref):
    for half, ref in enumerate((own_ref, other_ref)):
        for k in range(16):
            at = slice((half * 16 + k) * BLK, (half * 16 + k + 1) * BLK)
            rows = in_features(jnp.concatenate([ref[k, 0], ref[k, 1]], 0))
            f_ref[at, :] = jnp.transpose(rows).astype(jnp.bfloat16)
            a, b, c = split3(ref[k, 2])
            d_ref[:, at] = jnp.concatenate([a, b, c, jnp.zeros_like(a)], 0).astype(jnp.bfloat16)


def product_kernel(f_ref, d_ref, s_ref, out_ref, g_ref, acc_ref):
    n_s = s_ref.shape[0]
    for k in range(n_s):
        g_ref[:, k * BLK : (k + 1) * BLK] = out_features(s_ref[k, :8, :]).astype(jnp.bfloat16)
    acc_ref[...] = jnp.zeros_like(acc_ref)

    def step(i, carry):
        rows = pl.ds(pl.multiple_of(i * T_STEP, T_STEP), T_STEP)
        for j in range(n_s * BLK // S_TILE):
            at = slice(j * S_TILE, (j + 1) * S_TILE)
            total = acc_ref[:, at]
            for t in range(T_STEP // T_TILE):
                here = pl.ds(pl.multiple_of(i * T_STEP + t * T_TILE, T_TILE), T_TILE)
                d2 = jnp.dot(f_ref[here, :], g_ref[:, at], preferred_element_type=jnp.float32)
                neg = -HALF - lax.rsqrt(lax.rsqrt(d2 * d2))
                value = (neg * neg + REST) * jnp.exp2(neg)
                high = value.astype(jnp.bfloat16)
                low = (value - high.astype(jnp.float32)).astype(jnp.bfloat16)
                weights = d_ref[:, here]
                total = total + (
                    jnp.dot(weights, high, preferred_element_type=jnp.float32)
                    + jnp.dot(weights, low, preferred_element_type=jnp.float32)
                )
            acc_ref[:, at] = total
        return carry

    lax.fori_loop(0, f_ref.shape[0] // T_STEP, step, 0)
    total = acc_ref[0:4, :] + acc_ref[4:8, :] + acc_ref[8:12, :]
    for k in range(n_s):
        for to in range(n_s):
            out_ref[to, k, :, :] = total[:, k * BLK : (k + 1) * BLK]


def to_lanes(column):
    row = lax.broadcasted_iota(jnp.int32, (16, BLK), 0)
    lane = lax.broadcasted_iota(jnp.int32, (16, BLK), 1)
    return jnp.sum(jnp.where(row == lane, column, 0.0), axis=0, keepdims=True)


def to_column(lanes):
    row = lax.broadcasted_iota(jnp.int32, (16, BLK), 0)
    lane = lax.broadcasted_iota(jnp.int32, (16, BLK), 1)
    return jnp.sum(jnp.where(row == lane, lanes, 0.0), axis=1, keepdims=True)


def start_kernel(ls_ref, pts_ref, res_ref, dir_ref, to_yx_ref, to_z_ref, ls, pts, res, direct, sems):
    copies = [
        pltpu.make_async_copy(source, target, sems.at[k])
        for k, (source, target) in enumerate(
            ((ls_ref, ls), (pts_ref, pts), (dir_ref, direct), (res_ref, res))
        )
    ]
    for copy in copies:
        copy.start()
    for copy in copies:
        copy.wait()
    row = lax.broadcasted_iota(jnp.int32, (8, 8), 0)
    lane = lax.broadcasted_iota(jnp.int32, (8, 8), 1)
    scale = jnp.sum(jnp.where(row == lane, ls[...], 0.0), axis=1, keepdims=True)
    scaled = pts[...] / scale * UNIT
    direction, residual = direct[...], res[...]
    for k in range(16):
        to_yx_ref[k, 0:8, :] = scaled
        to_yx_ref[k, 8:12, :] = direction
        to_yx_ref[k, 12:16, :] = residual
        to_z_ref[k, 0] = scaled[0:4]
        to_z_ref[k, 1] = scaled[4:8]
        to_z_ref[k, 2] = direction


def sums_kernel(at_ref, sv_ref, nv_ref, parts_ref, s_ref, own_ref, out_ref, image_ref):
    front, noise = sv_ref[0] * FRONT, nv_ref[0]
    rr, curv, cross, square = (jnp.zeros((4, BLK), jnp.float32) for _ in range(4))
    for k in range(16):
        applied = parts_ref[0, k]
        for source in range(1, 16):
            applied = applied + parts_ref[source, k]
        s_dir, s_res = s_ref[k, 8:12, :], s_ref[k, 12:16, :]
        image = front * applied + noise * s_dir
        image_ref[k] = image
        rr, curv = rr + s_res * s_res, curv + s_dir * image
        cross, square = cross + s_res * image, square + image * image
    own_ref[...] = image_ref[at_ref[0]]
    column = jnp.sum(jnp.concatenate([rr, curv, cross, square], 0), axis=1, keepdims=True)
    lanes = to_lanes(column)
    for to in range(32):
        out_ref[to] = lanes


def end_kernel(sums_ref, own_ref, sol_ref, res_ref, dir_ref, new_sol_ref, new_res_ref, new_dir_ref):
    total = sums_ref[0]
    for k in range(1, 32):
        total = total + sums_ref[k]
    column = to_column(total)
    old_rr, curv, cross, square = (column[4 * k : 4 * k + 4] for k in range(4))
    alpha = old_rr / curv
    new_rr = old_rr - 2.0 * alpha * cross + alpha * alpha * square
    direction = dir_ref[...]
    new_residual = res_ref[...] - alpha * own_ref[...]
    new_sol_ref[...] = sol_ref[...] + alpha * direction
    new_res_ref[...] = new_residual
    new_dir_ref[...] = new_residual + (new_rr / old_rr) * direction


def call(body, shapes, where, scratch=(), entries=0, limit=40):
    spec = {
        "s": pl.BlockSpec(memory_space=pltpu.SMEM),
        "v": pl.BlockSpec(memory_space=pltpu.VMEM),
        "a": pl.BlockSpec(memory_space=pl.ANY),
    }
    return pl.pallas_call(
        body,
        out_shape=[jax.ShapeDtypeStruct(s, t) for s, t in shapes],
        in_specs=[spec[w] for w in where],
        out_specs=[pl.BlockSpec(memory_space=pltpu.VMEM) for _ in shapes],
        scratch_shapes=[x if hasattr(x, "dtype") else pltpu.VMEM(*x) for x in scratch],
        compiler_params=pltpu.CompilerParams(vmem_limit_bytes=limit * 1024 * 1024),
        cost_estimate=pl.CostEstimate(
            flops=entries * 192, bytes_accessed=0, transcendentals=entries * 2
        ),
    )


AXIS = "d"
YS, XS, ZS, CS = (2, 3, 0, 1), (2, 3, 0, 1), tuple((8 + k) % 16 for k in range(16)), (0, 1)


def flat(y, x, z, c):
    return ((y * 4 + x) * 16 + z) * 2 + c


ALONG_Z = [[flat(y, x, z, c) for z in ZS] for y in YS for x in XS for c in CS]
ALONG_YX = [[flat(y, x, z, c) for y in YS for x in XS] for z in ZS for c in CS]
ALONG_ZC = [[flat(y, x, z, c) for z in ZS for c in CS] for y in YS for x in XS]


def share(x, groups):
    return lax.all_to_all(x, AXIS, 0, 0, axis_index_groups=groups)


def on_device(points, lengthscale, signal_var, noise_var, solution, residual, direction):
    f32, bf16 = jnp.float32, jnp.bfloat16
    here = lax.axis_index(AXIS)
    place = ((here // 128 + 2) % 4 * 4 + (here // 32 + 2) % 4)[None]
    to_yx, to_z = call(
        start_kernel,
        [((16, 16, BLK), f32), ((16, 3, 4, BLK), f32)],
        "aaaa",
        [((1, 8), f32), ((8, BLK), f32), ((4, BLK), f32), ((4, BLK), f32), pltpu.SemaphoreType.DMA((4,))],
        limit=60,
    )(lengthscale[None], points, residual, direction)
    with jax.named_scope("gather_in_points"):
        t_own = share(to_z, ALONG_Z)
        t_other = lax.ppermute(t_own, AXIS, [(i, i ^ 1) for i in range(512)])
    with jax.named_scope("gather_out_points"):
        s_blocks = share(to_yx, ALONG_YX)
    n_t, n_s = 32 * BLK, 16 * BLK
    rows, weights = call(
        prepare_kernel, [((n_t, FEAT), bf16), ((16, n_t), bf16)], "vv", entries=n_t * 256
    )(t_own, t_other)
    (parts,) = call(
        product_kernel,
        [((16, 16, 4, BLK), f32)],
        "vvv",
        [((FEAT, n_s), bf16), ((16, n_s), f32)],
        n_t * n_s,
    )(rows, weights, s_blocks)
    with jax.named_scope("sum_partial_images"):
        parts = share(parts, ALONG_YX)
    own, to_zc = call(
        sums_kernel, [((4, BLK), f32), ((32, 1, BLK), f32)], "sssvv", [((16, 4, BLK), f32)]
    )(place, signal_var, noise_var, parts, s_blocks)
    with jax.named_scope("sum_scalars"):
        sums = share(to_zc, ALONG_ZC)
    return tuple(
        call(end_kernel, [((4, BLK), f32)] * 3, "vvvvv")(sums, own, solution, residual, direction)
    )


def solution(mesh):
    line = Mesh(mesh.devices.reshape(-1), (AXIS,))
    cut = P(None, AXIS)
    return jax.shard_map(
        on_device,
        mesh=line,
        in_specs=(cut, P(), P(), P(), cut, cut, cut),
        out_specs=(cut, cut, cut),
        check_vma=False,
    )
```

```python
import functools
import math

import jax
import jax.numpy as jnp
from jax import lax
from jax.experimental import pallas as pl
from jax.experimental.pallas import tpu as pltpu
from jax.sharding import Mesh, PartitionSpec as P

BLK = 128
LN2 = math.log(2.0)
UNIT = math.sqrt(5.0) / LN2
HALF = 1.5 / LN2
REST = 3.0 / LN2**2 - HALF**2
FRONT = LN2**2 / 3.0 * 2.0**HALF
FEAT = 64
S_TILE = 256
T_STEP = 4096
T_TILE = 256


def round16(x):
    return x.astype(jnp.bfloat16).astype(jnp.float32)


def split3(x):
    first = round16(x)
    rest = x - first
    second = round16(rest)
    return first, second, round16(rest - second)


def norm_rows(pts, flip):
    parts = split3(jnp.sum(pts * pts, axis=0, keepdims=True))
    row = lax.broadcasted_iota(jnp.int32, pts.shape, 0)
    at = 3 if flip else 0
    out = jnp.where((row >= 3 - at) & (row < 6 - at), 1.0, 0.0)
    for k in range(3):
        out = jnp.where(row == at + k, parts[k], out)
    return out


def out_features(pts):
    a, b, c = split3(pts)
    return jnp.concatenate([a, b, c, a, b, a, norm_rows(pts, False), jnp.zeros_like(pts)], 0)


def in_features(pts):
    a, b, c = split3(-2.0 * pts)
    return jnp.concatenate([a, a, a, b, b, c, norm_rows(pts, True), jnp.zeros_like(pts)], 0)


def prepare_kernel(own_ref, other_ref, f_ref, d_ref):
    for half, ref in enumerate((own_ref, other_ref)):
        for k in range(16):
            at = slice((half * 16 + k) * BLK, (half * 16 + k + 1) * BLK)
            rows = in_features(jnp.concatenate([ref[k, 0], ref[k, 1]], 0))
            f_ref[at, :] = jnp.transpose(rows).astype(jnp.bfloat16)
            a, b, c = split3(ref[k, 2])
            d_ref[:, at] = jnp.concatenate([a, b, c, jnp.zeros_like(a)], 0).astype(jnp.bfloat16)


def product_kernel(f_ref, d_ref, s_ref, out_ref, g_ref, acc_ref):
    n_s = s_ref.shape[0]
    for k in range(n_s):
        g_ref[:, k * BLK : (k + 1) * BLK] = out_features(s_ref[k, :8, :]).astype(jnp.bfloat16)
    acc_ref[...] = jnp.zeros_like(acc_ref)

    def step(i, carry):
        rows = pl.ds(pl.multiple_of(i * T_STEP, T_STEP), T_STEP)
        for j in range(n_s * BLK // S_TILE):
            at = slice(j * S_TILE, (j + 1) * S_TILE)
            total = acc_ref[:, at]
            for t in range(T_STEP // T_TILE):
                here = pl.ds(pl.multiple_of(i * T_STEP + t * T_TILE, T_TILE), T_TILE)
                d2 = jnp.dot(f_ref[here, :], g_ref[:, at], preferred_element_type=jnp.float32)
                neg = -HALF - lax.rsqrt(lax.rsqrt(d2 * d2))
                value = (neg * neg + REST) * jnp.exp2(neg)
                high = value.astype(jnp.bfloat16)
                low = (value - high.astype(jnp.float32)).astype(jnp.bfloat16)
                weights = d_ref[:, here]
                total = total + (
                    jnp.dot(weights, high, preferred_element_type=jnp.float32)
                    + jnp.dot(weights, low, preferred_element_type=jnp.float32)
                )
            acc_ref[:, at] = total
        return carry

    lax.fori_loop(0, f_ref.shape[0] // T_STEP, step, 0)
    total = acc_ref[0:4, :] + acc_ref[4:8, :] + acc_ref[8:12, :]
    for k in range(n_s):
        for to in range(n_s):
            out_ref[to, k, :, :] = total[:, k * BLK : (k + 1) * BLK]


def to_lanes(column):
    row = lax.broadcasted_iota(jnp.int32, (16, BLK), 0)
    lane = lax.broadcasted_iota(jnp.int32, (16, BLK), 1)
    return jnp.sum(jnp.where(row == lane, column, 0.0), axis=0, keepdims=True)


def to_column(lanes):
    row = lax.broadcasted_iota(jnp.int32, (16, BLK), 0)
    lane = lax.broadcasted_iota(jnp.int32, (16, BLK), 1)
    return jnp.sum(jnp.where(row == lane, lanes, 0.0), axis=1, keepdims=True)


def start_kernel(ls_ref, pts_ref, res_ref, dir_ref, to_yx_ref, to_z_ref, ls, pts, res, direct, sems):
    copies = [
        pltpu.make_async_copy(source, target, sems.at[k])
        for k, (source, target) in enumerate(
            ((ls_ref, ls), (pts_ref, pts), (dir_ref, direct), (res_ref, res))
        )
    ]
    for copy in copies:
        copy.start()
    for copy in copies:
        copy.wait()
    row = lax.broadcasted_iota(jnp.int32, (8, 8), 0)
    lane = lax.broadcasted_iota(jnp.int32, (8, 8), 1)
    scale = jnp.sum(jnp.where(row == lane, ls[...], 0.0), axis=1, keepdims=True)
    scaled = pts[...] / scale * UNIT
    direction, residual = direct[...], res[...]
    for k in range(16):
        to_yx_ref[k, 0:8, :] = scaled
        to_yx_ref[k, 8:12, :] = direction
        to_yx_ref[k, 12:16, :] = residual
        to_z_ref[k, 0] = scaled[0:4]
        to_z_ref[k, 1] = scaled[4:8]
        to_z_ref[k, 2] = direction


def sums_kernel(at_ref, sv_ref, nv_ref, parts_ref, s_ref, own_ref, out_ref, image_ref):
    front, noise = sv_ref[0] * FRONT, nv_ref[0]
    rr, curv, cross, square = (jnp.zeros((4, BLK), jnp.float32) for _ in range(4))
    for k in range(16):
        applied = parts_ref[0, k]
        for source in range(1, 16):
            applied = applied + parts_ref[source, k]
        s_dir, s_res = s_ref[k, 8:12, :], s_ref[k, 12:16, :]
        image = front * applied + noise * s_dir
        image_ref[k] = image
        rr, curv = rr + s_res * s_res, curv + s_dir * image
        cross, square = cross + s_res * image, square + image * image
    own_ref[...] = image_ref[at_ref[0]]
    column = jnp.sum(jnp.concatenate([rr, curv, cross, square], 0), axis=1, keepdims=True)
    lanes = to_lanes(column)
    for to in range(32):
        out_ref[to] = lanes


def end_kernel(sums_ref, own_ref, sol_ref, res_ref, dir_ref, new_sol_ref, new_res_ref, new_dir_ref):
    total = sums_ref[0]
    for k in range(1, 32):
        total = total + sums_ref[k]
    column = to_column(total)
    old_rr, curv, cross, square = (column[4 * k : 4 * k + 4] for k in range(4))
    alpha = old_rr / curv
    new_rr = old_rr - 2.0 * alpha * cross + alpha * alpha * square
    direction = dir_ref[...]
    new_residual = res_ref[...] - alpha * own_ref[...]
    new_sol_ref[...] = sol_ref[...] + alpha * direction
    new_res_ref[...] = new_residual
    new_dir_ref[...] = new_residual + (new_rr / old_rr) * direction


def call(body, shapes, where, scratch=(), entries=0, limit=40):
    spec = {
        "s": pl.BlockSpec(memory_space=pltpu.SMEM),
        "v": pl.BlockSpec(memory_space=pltpu.VMEM),
        "a": pl.BlockSpec(memory_space=pl.ANY),
    }
    return pl.pallas_call(
        body,
        out_shape=[x if hasattr(x, "memory_space") else jax.ShapeDtypeStruct(*x) for x in shapes],
        in_specs=[spec[w] for w in where],
        out_specs=[pl.BlockSpec(memory_space=pltpu.VMEM) for _ in shapes],
        scratch_shapes=[x if hasattr(x, "dtype") else pltpu.VMEM(*x) for x in scratch],
        compiler_params=pltpu.CompilerParams(vmem_limit_bytes=limit * 1024 * 1024),
        cost_estimate=pl.CostEstimate(
            flops=entries * 192, bytes_accessed=0, transcendentals=entries * 2
        ),
    )


AXIS = "d"
YS, XS, ZS, CS = (2, 3, 0, 1), (2, 3, 0, 1), tuple((8 + k) % 16 for k in range(16)), (0, 1)


def flat(y, x, z, c):
    return ((y * 4 + x) * 16 + z) * 2 + c


ALONG_Z = [[flat(y, x, z, c) for z in ZS] for y in YS for x in XS for c in CS]
ALONG_YX = [[flat(y, x, z, c) for y in YS for x in XS] for z in ZS for c in CS]
DIAGONAL_YX = [[flat((2 + k) % 4, (2 + k // 4 + k) % 4, z, c) for k in range(16)] for z in ZS for c in CS]
ALONG_ZC = [[flat(y, x, z, c) for z in ZS for c in CS] for y in YS for x in XS]


def share(x, groups):
    return lax.all_to_all(x, AXIS, 0, 0, axis_index_groups=groups)


def on_device(points, lengthscale, signal_var, noise_var, solution, residual, direction):
    f32, bf16 = jnp.float32, jnp.bfloat16
    here = lax.axis_index(AXIS)
    place = ((here // 128 + 2) % 4 * 4 + (here // 32 + 2) % 4)[None]
    to_yx, to_z = call(
        start_kernel,
        [pltpu.VMEM((16, 16, BLK), f32), pltpu.VMEM((16, 3, 4, BLK), f32)],
        "aaaa",
        [((1, 8), f32), ((8, BLK), f32), ((4, BLK), f32), ((4, BLK), f32), pltpu.SemaphoreType.DMA((4,))],
        limit=60,
    )(lengthscale[None], points, residual, direction)
    with jax.named_scope("gather_in_points"):
        t_own = share(to_z, ALONG_Z)
        t_other = lax.ppermute(t_own, AXIS, [(i, i ^ 1) for i in range(512)])
    with jax.named_scope("gather_out_points"):
        s_blocks = share(to_yx, ALONG_YX)
    n_t, n_s = 32 * BLK, 16 * BLK
    rows, weights = call(
        prepare_kernel, [pltpu.VMEM((n_t, FEAT), bf16), pltpu.VMEM((16, n_t), bf16)], "vv", entries=n_t * 256
    )(t_own, t_other)
    (parts,) = call(
        product_kernel,
        [pltpu.VMEM((16, 16, 4, BLK), f32)],
        "vvv",
        [((FEAT, n_s), bf16), ((16, n_s), f32)],
        n_t * n_s,
    )(rows, weights, s_blocks)
    with jax.named_scope("sum_partial_images"):
        parts = share(parts, DIAGONAL_YX)
    own, to_zc = call(
        sums_kernel, [pltpu.VMEM((4, BLK), f32), pltpu.VMEM((32, 1, BLK), f32)], "sssvv", [((16, 4, BLK), f32)]
    )(place, signal_var, noise_var, parts, s_blocks)
    with jax.named_scope("sum_scalars"):
        sums = share(to_zc, ALONG_ZC)
    return tuple(
        call(end_kernel, [((4, BLK), f32)] * 3, "vvvvv")(sums, own, solution, residual, direction)
    )


def solution(mesh):
    line = Mesh(mesh.devices.reshape(-1), (AXIS,))
    cut = P(None, AXIS)
    return jax.shard_map(
        on_device,
        mesh=line,
        in_specs=(cut, P(), P(), P(), cut, cut, cut),
        out_specs=(cut, cut, cut),
        check_vma=False,
    )
```

```python
import functools
import math

import jax
import jax.numpy as jnp
from jax import lax
from jax.experimental import pallas as pl
from jax.experimental.pallas import tpu as pltpu
from jax.sharding import Mesh, PartitionSpec as P

BLK = 128
LN2 = math.log(2.0)
UNIT = math.sqrt(5.0) / LN2
HALF = 1.5 / LN2
REST = 3.0 / LN2**2 - HALF**2
FRONT = LN2**2 / 3.0 * 2.0**HALF
FEAT = 64
S_TILE = 256
T_STEP = 4096
T_TILE = 128


def round16(x):
    return x.astype(jnp.bfloat16).astype(jnp.float32)


def split3(x):
    first = round16(x)
    rest = x - first
    second = round16(rest)
    return first, second, round16(rest - second)


def norm_rows(pts, flip):
    parts = split3(jnp.sum(pts * pts, axis=0, keepdims=True))
    row = lax.broadcasted_iota(jnp.int32, pts.shape, 0)
    at = 3 if flip else 0
    out = jnp.where((row >= 3 - at) & (row < 6 - at), 1.0, 0.0)
    for k in range(3):
        out = jnp.where(row == at + k, parts[k], out)
    return out


def out_features(pts):
    a, b, c = split3(pts)
    return jnp.concatenate([a, b, c, a, b, a, norm_rows(pts, False), jnp.zeros_like(pts)], 0)


def in_features(pts):
    a, b, c = split3(-2.0 * pts)
    return jnp.concatenate([a, a, a, b, b, c, norm_rows(pts, True), jnp.zeros_like(pts)], 0)


def prepare_kernel(own_ref, other_ref, f_ref, d_ref):
    for half, ref in enumerate((own_ref, other_ref)):
        for k in range(16):
            at = slice((half * 16 + k) * BLK, (half * 16 + k + 1) * BLK)
            rows = in_features(jnp.concatenate([ref[k, 0], ref[k, 1]], 0))
            f_ref[at, :] = jnp.transpose(rows).astype(jnp.bfloat16)
            a, b, c = split3(ref[k, 2])
            d_ref[:, at] = jnp.concatenate([a, b, c, jnp.zeros_like(a)], 0).astype(jnp.bfloat16)


def product_kernel(f_ref, d_ref, s_ref, out_ref, g_ref, acc_ref):
    n_s = s_ref.shape[0]
    for k in range(n_s):
        g_ref[:, k * BLK : (k + 1) * BLK] = out_features(s_ref[k, :8, :]).astype(jnp.bfloat16)
    acc_ref[...] = jnp.zeros_like(acc_ref)

    def step(i, carry):
        rows = pl.ds(pl.multiple_of(i * T_STEP, T_STEP), T_STEP)
        for j in range(n_s * BLK // S_TILE):
            at = slice(j * S_TILE, (j + 1) * S_TILE)
            total = acc_ref[:, at]
            for t in range(T_STEP // T_TILE):
                here = pl.ds(pl.multiple_of(i * T_STEP + t * T_TILE, T_TILE), T_TILE)
                d2 = jnp.dot(f_ref[here, :], g_ref[:, at], preferred_element_type=jnp.float32)
                neg = -HALF - lax.rsqrt(lax.rsqrt(d2 * d2))
                value = (neg * neg + REST) * jnp.exp2(neg)
                high = value.astype(jnp.bfloat16)
                low = (value - high.astype(jnp.float32)).astype(jnp.bfloat16)
                weights = d_ref[:, here]
                total = total + (
                    jnp.dot(weights, high, preferred_element_type=jnp.float32)
                    + jnp.dot(weights, low, preferred_element_type=jnp.float32)
                )
            acc_ref[:, at] = total
        return carry

    lax.fori_loop(0, f_ref.shape[0] // T_STEP, step, 0)
    total = acc_ref[0:4, :] + acc_ref[4:8, :] + acc_ref[8:12, :]
    for k in range(n_s):
        for to in range(n_s):
            out_ref[to, k, :, :] = total[:, k * BLK : (k + 1) * BLK]


def to_lanes(column):
    row = lax.broadcasted_iota(jnp.int32, (16, BLK), 0)
    lane = lax.broadcasted_iota(jnp.int32, (16, BLK), 1)
    return jnp.sum(jnp.where(row == lane, column, 0.0), axis=0, keepdims=True)


def to_column(lanes):
    row = lax.broadcasted_iota(jnp.int32, (16, BLK), 0)
    lane = lax.broadcasted_iota(jnp.int32, (16, BLK), 1)
    return jnp.sum(jnp.where(row == lane, lanes, 0.0), axis=1, keepdims=True)


def start_kernel(ls_ref, pts_ref, res_ref, dir_ref, to_yx_ref, to_z_ref, ls, pts, res, direct, sems):
    copies = [
        pltpu.make_async_copy(source, target, sems.at[k])
        for k, (source, target) in enumerate(
            ((ls_ref, ls), (pts_ref, pts), (dir_ref, direct), (res_ref, res))
        )
    ]
    for copy in copies:
        copy.start()
    for copy in copies:
        copy.wait()
    row = lax.broadcasted_iota(jnp.int32, (8, 8), 0)
    lane = lax.broadcasted_iota(jnp.int32, (8, 8), 1)
    scale = jnp.sum(jnp.where(row == lane, ls[...], 0.0), axis=1, keepdims=True)
    scaled = pts[...] / scale * UNIT
    direction, residual = direct[...], res[...]
    for k in range(16):
        to_yx_ref[k, 0:8, :] = scaled
        to_yx_ref[k, 8:12, :] = direction
        to_yx_ref[k, 12:16, :] = residual
        to_z_ref[k, 0] = scaled[0:4]
        to_z_ref[k, 1] = scaled[4:8]
        to_z_ref[k, 2] = direction


def sums_kernel(at_ref, sv_ref, nv_ref, parts_ref, s_ref, own_ref, out_ref, image_ref):
    front, noise = sv_ref[0] * FRONT, nv_ref[0]
    rr, curv, cross, square = (jnp.zeros((4, BLK), jnp.float32) for _ in range(4))
    for k in range(16):
        applied = parts_ref[0, k]
        for source in range(1, 16):
            applied = applied + parts_ref[source, k]
        s_dir, s_res = s_ref[k, 8:12, :], s_ref[k, 12:16, :]
        image = front * applied + noise * s_dir
        image_ref[k] = image
        rr, curv = rr + s_res * s_res, curv + s_dir * image
        cross, square = cross + s_res * image, square + image * image
    own_ref[...] = image_ref[at_ref[0]]
    column = jnp.sum(jnp.concatenate([rr, curv, cross, square], 0), axis=1, keepdims=True)
    lanes = to_lanes(column)
    for to in range(32):
        out_ref[to] = lanes


def end_kernel(sums_ref, own_ref, sol_ref, res_ref, dir_ref, new_sol_ref, new_res_ref, new_dir_ref):
    total = sums_ref[0]
    for k in range(1, 32):
        total = total + sums_ref[k]
    column = to_column(total)
    old_rr, curv, cross, square = (column[4 * k : 4 * k + 4] for k in range(4))
    alpha = old_rr / curv
    new_rr = old_rr - 2.0 * alpha * cross + alpha * alpha * square
    direction = dir_ref[...]
    new_residual = res_ref[...] - alpha * own_ref[...]
    new_sol_ref[...] = sol_ref[...] + alpha * direction
    new_res_ref[...] = new_residual
    new_dir_ref[...] = new_residual + (new_rr / old_rr) * direction


def call(body, shapes, where, scratch=(), entries=0, limit=40):
    spec = {
        "s": pl.BlockSpec(memory_space=pltpu.SMEM),
        "v": pl.BlockSpec(memory_space=pltpu.VMEM),
        "a": pl.BlockSpec(memory_space=pl.ANY),
    }
    return pl.pallas_call(
        body,
        out_shape=[x if hasattr(x, "memory_space") else jax.ShapeDtypeStruct(*x) for x in shapes],
        in_specs=[spec[w] for w in where],
        out_specs=[pl.BlockSpec(memory_space=pltpu.VMEM) for _ in shapes],
        scratch_shapes=[x if hasattr(x, "dtype") else pltpu.VMEM(*x) for x in scratch],
        compiler_params=pltpu.CompilerParams(vmem_limit_bytes=limit * 1024 * 1024),
        cost_estimate=pl.CostEstimate(
            flops=entries * 192, bytes_accessed=0, transcendentals=entries * 2
        ),
    )


AXIS = "d"
YS, XS, ZS, CS = (2, 3, 0, 1), (2, 3, 0, 1), tuple((8 + k) % 16 for k in range(16)), (0, 1)


def flat(y, x, z, c):
    return ((y * 4 + x) * 16 + z) * 2 + c


ALONG_Z = [[flat(y, x, z, c) for z in ZS] for y in YS for x in XS for c in CS]
DIAGONAL_YX = [[flat((2 + k) % 4, (2 + k // 4 + k) % 4, z, c) for k in range(16)] for z in ZS for c in CS]
ALONG_ZC = [[flat(y, x, z, c) for z in ZS for c in CS] for y in YS for x in XS]


def share(x, groups):
    return lax.all_to_all(x, AXIS, 0, 0, axis_index_groups=groups)


def on_device(points, lengthscale, signal_var, noise_var, solution, residual, direction):
    f32, bf16 = jnp.float32, jnp.bfloat16
    here = lax.axis_index(AXIS)
    from_y = (here // 128 + 2) % 4
    place = ((here // 32 + 2 - from_y) % 4 * 4 + from_y)[None]
    to_yx, to_z = call(
        start_kernel,
        [pltpu.VMEM((16, 16, BLK), f32), pltpu.VMEM((16, 3, 4, BLK), f32)],
        "aaaa",
        [((1, 8), f32), ((8, BLK), f32), ((4, BLK), f32), ((4, BLK), f32), pltpu.SemaphoreType.DMA((4,))],
        limit=60,
    )(lengthscale[None], points, residual, direction)
    with jax.named_scope("gather_in_points"):
        t_own = share(to_z, ALONG_Z)
        t_other = lax.ppermute(t_own, AXIS, [(i, i ^ 1) for i in range(512)])
    with jax.named_scope("gather_out_points"):
        s_blocks = share(to_yx, DIAGONAL_YX)
    n_t, n_s = 32 * BLK, 16 * BLK
    rows, weights = call(
        prepare_kernel, [pltpu.VMEM((n_t, FEAT), bf16), pltpu.VMEM((16, n_t), bf16)], "vv", entries=n_t * 256
    )(t_own, t_other)
    (parts,) = call(
        product_kernel,
        [pltpu.VMEM((16, 16, 4, BLK), f32)],
        "vvv",
        [((FEAT, n_s), bf16), ((16, n_s), f32)],
        n_t * n_s,
    )(rows, weights, s_blocks)
    with jax.named_scope("sum_partial_images"):
        parts = share(parts, DIAGONAL_YX)
    own, to_zc = call(
        sums_kernel, [pltpu.VMEM((4, BLK), f32), pltpu.VMEM((32, 1, BLK), f32)], "sssvv", [((16, 4, BLK), f32)]
    )(place, signal_var, noise_var, parts, s_blocks)
    with jax.named_scope("sum_scalars"):
        sums = share(to_zc, ALONG_ZC)
    return tuple(
        call(end_kernel, [((4, BLK), f32)] * 3, "vvvvv")(sums, own, solution, residual, direction)
    )


def solution(mesh):
    line = Mesh(mesh.devices.reshape(-1), (AXIS,))
    cut = P(None, AXIS)
    return jax.shard_map(
        on_device,
        mesh=line,
        in_specs=(cut, P(), P(), P(), cut, cut, cut),
        out_specs=(cut, cut, cut),
        check_vma=False,
    )
```

```python
import functools
import math

import jax
import jax.numpy as jnp
from jax import lax
from jax.experimental import pallas as pl
from jax.experimental.pallas import tpu as pltpu
from jax.sharding import Mesh, PartitionSpec as P

BLK = 128
LN2 = math.log(2.0)
UNIT = math.sqrt(5.0) / LN2
HALF = 1.5 / LN2
REST = 3.0 / LN2**2 - HALF**2
FRONT = LN2**2 / 3.0 * 2.0**HALF
FEAT = 64
S_TILE = 256
T_STEP = 4096
T_TILE = 128


def round16(x):
    return x.astype(jnp.bfloat16).astype(jnp.float32)


def split3(x):
    first = round16(x)
    rest = x - first
    second = round16(rest)
    return first, second, round16(rest - second)


def norm_rows(pts, flip):
    parts = split3(jnp.sum(pts * pts, axis=0, keepdims=True))
    row = lax.broadcasted_iota(jnp.int32, pts.shape, 0)
    at = 3 if flip else 0
    out = jnp.where((row >= 3 - at) & (row < 6 - at), 1.0, 0.0)
    for k in range(3):
        out = jnp.where(row == at + k, parts[k], out)
    return out


def out_features(pts):
    a, b, c = split3(pts)
    return jnp.concatenate([a, b, c, a, b, a, norm_rows(pts, False), jnp.zeros_like(pts)], 0)


def in_features(pts):
    a, b, c = split3(-2.0 * pts)
    return jnp.concatenate([a, a, a, b, b, c, norm_rows(pts, True), jnp.zeros_like(pts)], 0)


def prepare_kernel(own_ref, other_ref, f_ref, d_ref):
    for half, ref in enumerate((own_ref, other_ref)):
        for k in range(16):
            at = slice((half * 16 + k) * BLK, (half * 16 + k + 1) * BLK)
            rows = in_features(jnp.concatenate([ref[k, 0], ref[k, 1]], 0))
            f_ref[at, :] = jnp.transpose(rows).astype(jnp.bfloat16)
            a, b, c = split3(ref[k, 2])
            d_ref[:, at] = jnp.concatenate([a, b, c, jnp.zeros_like(a)], 0).astype(jnp.bfloat16)


def product_kernel(f_ref, d_ref, s_ref, out_ref, g_ref, acc_ref):
    n_s = s_ref.shape[0]
    for k in range(n_s):
        g_ref[:, k * BLK : (k + 1) * BLK] = out_features(s_ref[k, :8, :]).astype(jnp.bfloat16)
    acc_ref[...] = jnp.zeros_like(acc_ref)

    def step(i, carry):
        rows = pl.ds(pl.multiple_of(i * T_STEP, T_STEP), T_STEP)
        for j in range(n_s * BLK // S_TILE):
            at = slice(j * S_TILE, (j + 1) * S_TILE)
            total = acc_ref[:, at]
            for t in range(T_STEP // T_TILE):
                here = pl.ds(pl.multiple_of(i * T_STEP + t * T_TILE, T_TILE), T_TILE)
                d2 = jnp.dot(f_ref[here, :], g_ref[:, at], preferred_element_type=jnp.float32)
                neg = -HALF - lax.rsqrt(lax.rsqrt(d2 * d2))
                value = (neg * neg + REST) * jnp.exp2(neg)
                high = value.astype(jnp.bfloat16)
                low = (value - high.astype(jnp.float32)).astype(jnp.bfloat16)
                weights = d_ref[:, here]
                total = total + (
                    jnp.dot(weights, high, preferred_element_type=jnp.float32)
                    + jnp.dot(weights, low, preferred_element_type=jnp.float32)
                )
            acc_ref[:, at] = total
        return carry

    lax.fori_loop(0, f_ref.shape[0] // T_STEP, step, 0)
    total = acc_ref[0:4, :] + acc_ref[4:8, :] + acc_ref[8:12, :]
    for k in range(n_s):
        for to in range(n_s):
            out_ref[to, k, :, :] = total[:, k * BLK : (k + 1) * BLK]


def to_lanes(column):
    row = lax.broadcasted_iota(jnp.int32, (16, BLK), 0)
    lane = lax.broadcasted_iota(jnp.int32, (16, BLK), 1)
    return jnp.sum(jnp.where(row == lane, column, 0.0), axis=0, keepdims=True)


def to_column(lanes):
    row = lax.broadcasted_iota(jnp.int32, (16, BLK), 0)
    lane = lax.broadcasted_iota(jnp.int32, (16, BLK), 1)
    return jnp.sum(jnp.where(row == lane, lanes, 0.0), axis=1, keepdims=True)


def start_kernel(ls_ref, pts_ref, res_ref, dir_ref, to_yx_ref, to_z_ref, ls, pts, res, direct, sems):
    copies = [
        pltpu.make_async_copy(source, target, sems.at[k])
        for k, (source, target) in enumerate(
            ((ls_ref, ls), (pts_ref, pts), (dir_ref, direct), (res_ref, res))
        )
    ]
    for copy in copies:
        copy.start()
    for copy in copies:
        copy.wait()
    row = lax.broadcasted_iota(jnp.int32, (8, 8), 0)
    lane = lax.broadcasted_iota(jnp.int32, (8, 8), 1)
    scale = jnp.sum(jnp.where(row == lane, ls[...], 0.0), axis=1, keepdims=True)
    scaled = pts[...] / scale * UNIT
    direction, residual = direct[...], res[...]
    for k in range(16):
        to_yx_ref[k, 0:8, :] = scaled
        to_yx_ref[k, 8:12, :] = direction
        to_yx_ref[k, 12:16, :] = residual
        to_z_ref[k, 0] = scaled[0:4]
        to_z_ref[k, 1] = scaled[4:8]
        to_z_ref[k, 2] = direction


def sums_kernel(at_ref, sv_ref, nv_ref, parts_ref, s_ref, own_ref, out_ref, image_ref):
    front, noise = sv_ref[0] * FRONT, nv_ref[0]
    rr, curv, cross, square = (jnp.zeros((4, BLK), jnp.float32) for _ in range(4))
    for k in range(16):
        applied = parts_ref[0, k]
        for source in range(1, 16):
            applied = applied + parts_ref[source, k]
        s_dir, s_res = s_ref[k, 8:12, :], s_ref[k, 12:16, :]
        image = front * applied + noise * s_dir
        image_ref[k] = image
        rr, curv = rr + s_res * s_res, curv + s_dir * image
        cross, square = cross + s_res * image, square + image * image
    own_ref[...] = image_ref[at_ref[0]]
    column = jnp.sum(jnp.concatenate([rr, curv, cross, square], 0), axis=1, keepdims=True)
    lanes = to_lanes(column)
    for to in range(32):
        out_ref[to] = lanes


def end_kernel(sums_ref, own_ref, sol_ref, res_ref, dir_ref, new_sol_ref, new_res_ref, new_dir_ref):
    total = sums_ref[0]
    for k in range(1, 32):
        total = total + sums_ref[k]
    column = to_column(total)
    old_rr, curv, cross, square = (column[4 * k : 4 * k + 4] for k in range(4))
    alpha = old_rr / curv
    new_rr = old_rr - 2.0 * alpha * cross + alpha * alpha * square
    direction = dir_ref[...]
    new_residual = res_ref[...] - alpha * own_ref[...]
    new_sol_ref[...] = sol_ref[...] + alpha * direction
    new_res_ref[...] = new_residual
    new_dir_ref[...] = new_residual + (new_rr / old_rr) * direction


def call(body, shapes, where, scratch=(), entries=0, limit=40):
    spec = {
        "s": pl.BlockSpec(memory_space=pltpu.SMEM),
        "v": pl.BlockSpec(memory_space=pltpu.VMEM),
        "a": pl.BlockSpec(memory_space=pl.ANY),
    }
    return pl.pallas_call(
        body,
        out_shape=[x if hasattr(x, "memory_space") else jax.ShapeDtypeStruct(*x) for x in shapes],
        in_specs=[spec[w] for w in where],
        out_specs=[pl.BlockSpec(memory_space=pltpu.VMEM) for _ in shapes],
        scratch_shapes=[x if hasattr(x, "dtype") else pltpu.VMEM(*x) for x in scratch],
        compiler_params=pltpu.CompilerParams(vmem_limit_bytes=limit * 1024 * 1024),
        cost_estimate=pl.CostEstimate(
            flops=entries * 192, bytes_accessed=0, transcendentals=entries * 2
        ),
    )


AXIS = "d"
YS, XS, ZS, CS = (2, 3, 0, 1), (2, 3, 0, 1), tuple((9 + k) % 16 for k in range(16)), (0, 1)


def flat(y, x, z, c):
    return ((y * 4 + x) * 16 + z) * 2 + c


ALONG_Z = [[flat(y, x, z, c) for z in ZS] for y in YS for x in XS for c in CS]
DIAGONAL_YX = [[flat((2 + k) % 4, (2 + k // 4 + k) % 4, z, c) for k in range(16)] for z in ZS for c in CS]
ALONG_ZC = [[flat(y, x, z, c) for z in ZS for c in CS] for y in YS for x in XS]


def share(x, groups):
    return lax.all_to_all(x, AXIS, 0, 0, axis_index_groups=groups)


def on_device(points, lengthscale, signal_var, noise_var, solution, residual, direction):
    f32, bf16 = jnp.float32, jnp.bfloat16
    here = lax.axis_index(AXIS)
    from_y = (here // 128 + 2) % 4
    place = ((here // 32 + 2 - from_y) % 4 * 4 + from_y)[None]
    to_yx, to_z = call(
        start_kernel,
        [pltpu.VMEM((16, 16, BLK), f32), pltpu.VMEM((16, 3, 4, BLK), f32)],
        "aaaa",
        [((1, 8), f32), ((8, BLK), f32), ((4, BLK), f32), ((4, BLK), f32), pltpu.SemaphoreType.DMA((4,))],
        limit=60,
    )(lengthscale[None], points, residual, direction)
    with jax.named_scope("gather_in_points"):
        t_own = share(to_z, ALONG_Z)
        t_other = lax.ppermute(t_own, AXIS, [(i, i ^ 1) for i in range(512)])
    with jax.named_scope("gather_out_points"):
        s_blocks = share(to_yx, DIAGONAL_YX)
    n_t, n_s = 32 * BLK, 16 * BLK
    rows, weights = call(
        prepare_kernel, [pltpu.VMEM((n_t, FEAT), bf16), pltpu.VMEM((16, n_t), bf16)], "vv", entries=n_t * 256
    )(t_own, t_other)
    (parts,) = call(
        product_kernel,
        [pltpu.VMEM((16, 16, 4, BLK), f32)],
        "vvv",
        [((FEAT, n_s), bf16), ((16, n_s), f32)],
        n_t * n_s,
    )(rows, weights, s_blocks)
    with jax.named_scope("sum_partial_images"):
        parts = share(parts, DIAGONAL_YX)
    own, to_zc = call(
        sums_kernel, [pltpu.VMEM((4, BLK), f32), pltpu.VMEM((32, 1, BLK), f32)], "sssvv", [((16, 4, BLK), f32)]
    )(place, signal_var, noise_var, parts, s_blocks)
    with jax.named_scope("sum_scalars"):
        sums = share(to_zc, ALONG_ZC)
    return tuple(
        call(end_kernel, [((4, BLK), f32)] * 3, "vvvvv")(sums, own, solution, residual, direction)
    )


def solution(mesh):
    line = Mesh(mesh.devices.reshape(-1), (AXIS,))
    cut = P(None, AXIS)
    return jax.shard_map(
        on_device,
        mesh=line,
        in_specs=(cut, P(), P(), P(), cut, cut, cut),
        out_specs=(cut, cut, cut),
        check_vma=False,
    )
```
